512 devices in a mesh: dp: 128 (over y, x, z_lo, core), mp: 4 (over z_hi).
Axes of the slice: x: 4, y: 8, z: 8 (z_hi: 4, z_lo: 2; z = z_hi * 2 + z_lo), core: 2. Of those that a mesh axis runs over, the one named last changes fastest.
Arguments:
- inputs: bfloat16 [32768, 2560], P('dp', 'mp'), may hold values from -6 to 6
- out_grads: bfloat16 [32768, 2560], P('dp', 'mp'), may hold values from -6 to 6
- doc_lengths: int32 [128, 16], P('dp'), may hold values from 1 to 128, 256 in all within a row
- owners: int32 [4, 4], P('mp'), may hold values from 0 to 127, as said below
- basis_in: bfloat16 [81920, 2560], P('dp', 'mp'), may hold values from -0.25 to 0.25
- basis_out: bfloat16 [81920, 2560], P('dp', 'mp'), may hold values from -0.25 to 0.25
- eig_in: float32 [128, 2560], P('dp', 'mp'), may hold values from 0.25 to 2
- eig_out: float32 [128, 2560], P('dp', 'mp'), may hold values from 0.25 to 2
Outputs:
- update: bfloat16 [2560, 2560], P('mp', 'dp')
The draws below stay inside these ranges and needn't reach their ends.
Inputs may be any that keep to these rules, and one draw needn't show every extreme that they name: In each row the 4 owners are different dp indices.
All inputs are finite; a program needn't handle non-finite values.
Results may differ from the reference program's by a relative error of at most 0.013.
Values may be sent and summed in bfloat16 or wider, within the bound.
No kernel may reach another device: no remote copies, remote signals or barrier semaphores. Data moves between devices by JAX's collectives and lax.ppermute only.
A program may use at most 64 MiB of HBM per device.

```python
import math
import jax
import jax.numpy as jnp
import numpy as np
from jax import lax

WIN = 2560
BLOCK = 640
TOK_DEV = 256
DOCS = 16
NBLK = 4
TOKENS = 32768
N_DP = 128


def draw_owners(key, part):
    key = jax.random.fold_in(key, 7)
    row_keys = jax.random.split(key, NBLK)

    def one_row(row_key):
        return jax.random.permutation(row_key, N_DP)[:NBLK]
    return jax.vmap(one_row)(row_keys).astype(jnp.int32)


def shard_levels(key, shape, cuts, low, top_value):
    loudness, own = 1.0, jax.random.fold_in(key, 6)
    for position, parts in cuts:
        draws = jnp.exp(jax.random.uniform(jax.random.fold_in(own, position), (parts,), jnp.float32, low / len(cuts), top_value / len(cuts)))
        loudness = loudness * jnp.repeat(draws, shape[position] // parts).reshape([-1 if axis == position else 1 for axis in range(len(shape))])
    return loudness


def profile(number_of, total, most, skew):
    weights = [(1 << 20) // math.isqrt(standing ** skew) + 1 for standing in range(2, number_of + 1)]
    surplus, given = total - most - (number_of - 1), [1] * (number_of - 1)
    while surplus > 0:
        free = [i for i in range(number_of - 1) if given[i] < most]
        pool, budget = sum([weights[i] for i in free]), surplus
        for i in free:
            addition = min(most - given[i], max(1, budget * weights[i] // pool), surplus)
            given[i] = given[i] + addition
            surplus = surplus - addition
    return np.array([most] + given)


def uneven(stream_key, count, total, bound, skew):
    if count == 2:
        one = jax.random.randint(stream_key, (), max(1, total - bound), min(bound, total - 1) + 1)
        return jnp.stack([one, total - one])
    sizes = jnp.asarray(profile(count, total, bound, skew), jnp.int32)
    couples = (count - 1) // 2
    giver, sink = sizes[1:1 + 2 * couples:2], sizes[2:2 + 2 * couples:2]
    margin = jnp.minimum(giver - 1, bound - sink)
    moved = jax.random.randint(jax.random.fold_in(stream_key, 1), (couples,), 0, 1 << 20) % (margin + 1)
    sizes = sizes.at[1:1 + 2 * couples:2].set(giver - moved).at[2:2 + 2 * couples:2].set(sink + moved)
    return sizes[jax.random.permutation(jax.random.fold_in(stream_key, 2), count)]


def scatter_about(stream_key, dims, scale, reach, shards=(), kind=jnp.bfloat16):
    loudness = shard_levels(stream_key, dims, shards, -0.22, 0.18) if shards else 1.0
    values = jax.random.normal(stream_key, dims, jnp.float32) * scale * loudness
    return jnp.minimum(jnp.maximum(values, -reach), reach).astype(kind)


def setup_inputs(seed: int = 0) -> dict:
    arg_keys = jax.random.split(jax.random.key(seed), 9)
    inputs = scatter_about(arg_keys[0], (TOKENS, WIN), 1.0, 6.0, ((0, 128), (1, 4)))
    out_grads = scatter_about(arg_keys[1], (TOKENS, WIN), 1.0, 6.0, ((0, 128), (1, 4)))
    doc_lengths = jax.vmap(lambda own: uneven(own, DOCS, TOK_DEV, TOK_DEV // 2, 2))(jax.random.split(arg_keys[2], N_DP)).reshape((N_DP, DOCS)).astype(jnp.int32)
    owners = draw_owners(jax.random.fold_in(arg_keys[8], 71), 0)
    basis_in = scatter_about(arg_keys[4], (N_DP * BLOCK, WIN), BLOCK ** -0.5, 0.25, ((0, 128), (1, 4)))
    basis_out = scatter_about(arg_keys[5], (N_DP * BLOCK, WIN), BLOCK ** -0.5, 0.25, ((0, 128), (1, 4)))
    eig_in = jnp.clip(jnp.exp(math.log(2.0) - 2.0794415 * jax.random.uniform(arg_keys[6], (N_DP, WIN), jnp.float32) ** shard_levels(arg_keys[6], (N_DP, WIN), ((0, 128), (1, 4)), -0.2, 0.2)), 0.25, 2.0)
    eig_out = jnp.clip(jnp.exp(math.log(2.0) - 2.0794415 * jax.random.uniform(arg_keys[7], (N_DP, WIN), jnp.float32) ** shard_levels(arg_keys[7], (N_DP, WIN), ((0, 128), (1, 4)), -0.2, 0.2)), 0.25, 2.0)
    return dict(inputs=inputs, out_grads=out_grads, doc_lengths=doc_lengths, owners=owners, basis_in=basis_in, basis_out=basis_out, eig_in=eig_in, eig_out=eig_out)


DAMPING = 0.1


def token_weights(lengths):
    ends = jnp.cumsum(lengths)
    starts = ends - lengths
    positions = jnp.arange(TOK_DEV, dtype=jnp.int32)
    inside = (positions[:, None] >= starts[None, :]) & (positions[:, None] < ends[None, :])
    per_row = jnp.sum(jnp.where(inside, lengths[None, :], 0), axis=1)
    return 1.0 / (N_DP * per_row.astype(jnp.float32))


def precondition(gradient_tile, in_basis, out_basis, in_value, out_value):
    rotated = lax.dot_general(in_basis, gradient_tile, (((0,), (0,)), ((), ())), preferred_element_type=jnp.float32).astype(jnp.bfloat16)
    twice = jnp.dot(rotated, out_basis, preferred_element_type=jnp.float32)
    scaled = (twice / (in_value[:, None] * out_value[None, :] + DAMPING)).astype(jnp.bfloat16)
    returned = jnp.dot(in_basis, scaled, preferred_element_type=jnp.float32).astype(jnp.bfloat16)
    return lax.dot_general(returned, out_basis, (((1,), (1,)), ((), ())), preferred_element_type=jnp.float32).astype(jnp.bfloat16)


def reference(inputs, out_grads, doc_lengths, owners, basis_in, basis_out, eig_in, eig_out):
    input_rows = inputs.reshape(N_DP, TOK_DEV, WIN)
    grad_rows = out_grads.reshape(N_DP, TOK_DEV, WIN)

    def accumulate(total, pieces):
        own_inputs, own_grads, lengths = pieces
        weighted = (own_inputs.astype(jnp.float32) * token_weights(lengths)[:, None]).astype(jnp.bfloat16)
        partial_term = lax.dot_general(weighted, own_grads, (((0,), (0,)), ((), ())), preferred_element_type=jnp.float32)
        rounded = lax.optimization_barrier(partial_term.astype(jnp.bfloat16))
        return total + rounded.astype(jnp.float32), None

    total, unused = lax.scan(accumulate, jnp.zeros((WIN, WIN), jnp.float32), (input_rows, grad_rows, doc_lengths))
    gradient = total.astype(jnp.bfloat16)
    block_rows = []
    for row_block in range(NBLK):
        tiles = []
        offset = jnp.int32(row_block * BLOCK)
        for column_block in range(NBLK):
            column_offset = jnp.int32(column_block * BLOCK)
            owner_index = owners[row_block, column_block].astype(jnp.int32)
            in_basis = lax.dynamic_slice(basis_in, (owner_index * BLOCK, offset), (BLOCK, BLOCK))
            out_basis = lax.dynamic_slice(basis_out, (owner_index * BLOCK, column_offset), (BLOCK, BLOCK))
            in_value = lax.dynamic_slice(eig_in, (owner_index, offset), (1, BLOCK))[0]
            out_value = lax.dynamic_slice(eig_out, (owner_index, column_offset), (1, BLOCK))[0]
            gradient_tile = gradient[row_block * BLOCK:(row_block + 1) * BLOCK, column_block * BLOCK:(column_block + 1) * BLOCK]
            tiles.append(precondition(gradient_tile, in_basis, out_basis, in_value, out_value))
        block_rows.append(jnp.concatenate(tiles, axis=1))
    return jnp.concatenate(block_rows, axis=0)
```

```python
import jax
import jax.numpy as jnp
from jax import lax
from jax.sharding import Mesh
from jax.sharding import PartitionSpec as P

DAMPING = 0.1
SPLIT = (4, 2, 4, 2, 2, 4)
AXES = ("yj", "yh", "x", "zl", "c", "mp")
DP = AXES[:5]
ROW = ("x", "zl", "c")
NEXT_TO = [(0, 1), (1, 0), (2, 3), (3, 2)]
ACROSS = [(0, 3), (3, 0), (1, 2), (2, 1)]
PLACE = ((0, 2, 3, 1), (2, 0, 1, 3), (3, 1, 0, 2), (1, 3, 2, 0))
F32 = jnp.float32
BF16 = jnp.bfloat16


def token_weights(lengths, row_count, replicas):
    ends = jnp.cumsum(lengths)
    starts = ends - lengths
    positions = jnp.arange(row_count, dtype=jnp.int32)
    inside = (positions[:, None] >= starts[None, :]) & (positions[:, None] < ends[None, :])
    per_row = jnp.sum(jnp.where(inside, lengths[None, :], 0), axis=1)
    return 1.0 / (replicas * per_row.astype(F32))


def exchange(x, axes):
    return lax.all_to_all(x, axes, split_axis=0, concat_axis=0, tiled=True)


def pick(x, i):
    return lax.dynamic_index_in_dim(x, i, 0, keepdims=False)


def two_terms(v):
    high = lax.reduce_precision(v, 8, 7)
    return [high.astype(BF16), (v - high).astype(BF16)]


def partial_products(w, g):
    g2 = g.reshape(256, 2, 320).transpose(1, 0, 2)
    xp = lax.ppermute(w, "mp", NEXT_TO)
    gq = lax.ppermute(g2, "mp", ACROSS)
    xs = [lax.all_gather(v, "c", axis=0, tiled=True) for v in (w, xp)]
    gs = [exchange(v, "c").reshape(512, 320) for v in (g2, gq)]
    blocks = []
    for xm in xs:
        for gj in gs:
            d = lax.dot_general(gj, xm, (((0,), (0,)), ((), ())), preferred_element_type=F32)
            blocks.append(d.astype(BF16).reshape(4, 80, 640))
    return jnp.stack(blocks, axis=1)


def tile_of_gradient(parts):
    z = lax.axis_index("mp")
    summed = lax.psum_scatter(parts, "x", scatter_dimension=0, tiled=True)[0]
    other = lax.ppermute(summed[2:], "mp", NEXT_TO)
    four = jnp.concatenate([summed[:2], other], axis=0)
    places = jnp.asarray(PLACE, jnp.int32)[z]
    ordered = jnp.stack([pick(four, places[j]) for j in range(4)])
    received = exchange(ordered.reshape(16, 20, 640), ("yj", "yh", "zl"))
    piece = jnp.sum(received.astype(F32), axis=0).astype(BF16)
    spread = exchange(jnp.broadcast_to(piece[None], (16, 20, 640)), ("x", "yh", "zl"))
    return lax.all_gather(spread.reshape(320, 640), "c", axis=0, tiled=True)


def bases_of_tile(owners, u, v, ei, eo):
    z = lax.axis_index("mp")
    every = lax.all_gather(owners, "mp", axis=0, tiled=True)
    mine = owners[0]
    theirs = lax.dynamic_index_in_dim(every, z, 1, keepdims=False)
    small = jnp.stack(two_terms(ei[0]) + two_terms(eo[0]))
    sent = jnp.concatenate(
        [
            u.reshape(16, 40, 640),
            v.reshape(16, 40, 640),
            jnp.broadcast_to(small[None], (16, 4, 640)),
            jnp.zeros((16, 4, 640), BF16),
        ],
        axis=1,
    )
    row = exchange(sent, ROW)
    u_part = jnp.stack([pick(row, mine[j] % 16) for j in range(4)])
    v_part = exchange(jnp.stack([pick(row, theirs[m] % 16)[40:] for m in range(4)]), "mp")
    both = jnp.concatenate([u_part[:, :40], v_part[:, :40], u_part[:, 80:82], v_part[:, 42:44], u_part[:, 84:88]], axis=1)
    both = jnp.broadcast_to(both[:, None], (4, 2, 88, 640)).reshape(8, 88, 640)
    column = exchange(both, ("yj", "yh"))
    owner = pick(mine, lax.axis_index("yj"))
    whole = lax.all_gather(pick(column, owner // 16)[None], ROW, axis=0, tiled=True)
    u_tile = whole[:, :40].reshape(640, 640)
    v_tile = whole[:, 40:80].reshape(640, 640)
    small = whole[0, 80:84].astype(F32)
    return u_tile, v_tile, small[0] + small[1], small[2] + small[3]


def shards(inputs, out_grads, doc_lengths, owners, basis_in, basis_out, eig_in, eig_out):
    weights = token_weights(doc_lengths[0], inputs.shape[0], lax.axis_size(DP))
    weighted = (inputs.astype(F32) * weights[:, None]).astype(BF16)
    parts = partial_products(weighted, out_grads)
    u, v, ei, eo = bases_of_tile(owners, basis_in, basis_out, eig_in, eig_out)
    gt = tile_of_gradient(parts)
    first = (lax.axis_index(DP) % 32) * 20
    v_own = lax.dynamic_slice_in_dim(v, first, 20, 0)
    rotated = jnp.dot(gt, u, preferred_element_type=F32).astype(BF16)
    twice = lax.dot_general(v, rotated, (((0,), (0,)), ((), ())), preferred_element_type=F32)
    scaled = (twice / (eo[:, None] * ei[None, :] + DAMPING)).astype(BF16)
    back = jnp.dot(v_own, scaled, preferred_element_type=F32).astype(BF16)
    out = lax.dot_general(back, u, (((1,), (1,)), ((), ())), preferred_element_type=F32)
    return out.astype(BF16).T


def solution(mesh):
    fine = Mesh(mesh.devices.reshape(SPLIT), AXES)
    split = P(DP, "mp")
    placed = (split, split, P(DP, None), P("mp", None), split, split, split, split)
    return jax.shard_map(
        shards, mesh=fine, in_specs=placed, out_specs=P("mp", DP), check_vma=False
    )
```

```python
import jax
import jax.numpy as jnp
from jax import lax
from jax.experimental import pallas as pl
from jax.experimental.pallas import tpu as pltpu
from jax.sharding import Mesh
from jax.sharding import PartitionSpec as P

DAMPING = 0.1
SPLIT = (4, 2, 4, 2, 2, 4)
AXES = ("yj", "yh", "x", "zl", "c", "mp")
DP = AXES[:5]
ROW = ("yh", "x", "c")
COLUMN = ("yj", "zl")
F32 = jnp.float32
BF16 = jnp.bfloat16


def token_weights(lengths, row_count, replicas):
    ends = jnp.cumsum(lengths)
    starts = ends - lengths
    positions = jnp.arange(row_count, dtype=jnp.int32)
    inside = (positions[:, None] >= starts[None, :]) & (positions[:, None] < ends[None, :])
    per_row = jnp.sum(jnp.where(inside, lengths[None, :], 0), axis=1)
    return 1.0 / (replicas * per_row.astype(F32))


def exchange(x, axes):
    return lax.all_to_all(x, axes, split_axis=0, concat_axis=0, tiled=True)


def pool(x):
    return lax.all_gather(x, "c", axis=0, tiled=True)


def by_block(entries):
    z = lax.axis_index("mp")
    a, b, c, d = entries
    low, high = z % 2 == 1, z // 2 == 1
    a, b = jnp.where(low, b, a), jnp.where(low, a, b)
    c, d = jnp.where(low, d, c), jnp.where(low, c, d)
    a, c = jnp.where(high, c, a), jnp.where(high, a, c)
    b, d = jnp.where(high, d, b), jnp.where(high, b, d)
    return [a, b, c, d]


def two_terms(v):
    high = lax.reduce_precision(v, 8, 7)
    return jnp.stack([high.astype(BF16), (v - high).astype(BF16)])


def rows_sent(u, v, ei, eo):
    small = jnp.concatenate([two_terms(ei), two_terms(eo), jnp.zeros((4, 640), BF16)])
    small = jnp.broadcast_to(small[None], (16, 8, 640))
    return jnp.concatenate([u.reshape(16, 40, 640), v.reshape(16, 40, 640), small], axis=1)


def product(g, x):
    d = lax.dot_general(g, x, (((0,), (0,)), ((), ())), preferred_element_type=F32)
    return d.astype(BF16).reshape(4, 1, 80, 640)


def shift(x, distance):
    return lax.ppermute(x, "mp", [(i, i ^ distance) for i in range(4)])


def swapped(inputs, out_grads, owners, lengths, sent):
    weights = token_weights(lengths, inputs.shape[0], lax.axis_size(DP))[:, None]

    def weigh(x):
        return pool((x.astype(F32) * weights).astype(BF16))

    g = pool(out_grads)
    g = jnp.where(lax.axis_index("c") == 0, g[:, :320], g[:, 320:])
    row = exchange(sent, ROW)
    x_next = shift(inputs, 1)
    g_across = shift(g, 3)
    x = weigh(inputs)
    near = product(g, x)
    owners, near = lax.optimization_barrier((owners, near))
    rows = jnp.stack([owners] + [shift(owners, d) for d in (1, 2, 3)])
    row, x_next, g_across, rows = lax.optimization_barrier((row, x_next, g_across, rows))
    x_next = weigh(x_next)
    parts = [near, product(g_across, x), product(g, x_next), product(g_across, x_next)]
    return row, rows, jnp.concatenate(parts, axis=1)


def row_sums(parts):
    summed = lax.psum_scatter(parts, "x", scatter_dimension=0, tiled=True)[0]
    back = shift(summed[2:], 1)
    return jnp.stack(by_block([summed[0], back[0], back[1], summed[1]]))


def tile_of_gradient(four):
    received = exchange(four.reshape(16, 20, 640), ("yj", "yh", "zl"))
    piece = jnp.sum(received.astype(F32), axis=0).astype(BF16)
    spread = exchange(jnp.broadcast_to(piece[None], (16, 20, 640)), ("x", "yh", "zl"))
    return pool(spread.reshape(320, 640))


def within_row(owner):
    return ((owner >> 4) & 1) * 8 + ((owner >> 2) & 3) * 2 + (owner & 1)


def within_column(owner):
    return (owner >> 5) * 2 + ((owner >> 1) & 1)


def choose_v(row, rows, z):
    def body(rows_ref, z_ref, row_ref, out_ref):
        here = z_ref[0]
        for m in range(4):
            source = within_row(rows_ref[(here ^ m) * 4 + here])
            out_ref[m] = row_ref[source, 40:88, :]

    return on_scalars(body, (rows.reshape(16), z), (row,), (4, 48, 640))


def choose_both(row, v_part, mine):
    def body(mine_ref, row_ref, v_ref, out_ref):
        for j in range(4):
            source = within_row(mine_ref[j])
            for half in range(2):
                out_ref[2 * j + half, 0:40, :] = row_ref[source, 0:40, :]
                out_ref[2 * j + half, 40:80, :] = v_ref[j, 0:40, :]
                out_ref[2 * j + half, 80:82, :] = row_ref[source, 80:82, :]
                out_ref[2 * j + half, 82:88, :] = v_ref[j, 42:48, :]

    return on_scalars(body, (mine,), (row, v_part), (8, 88, 640))


def choose_one(column, mine, tile):
    def body(mine_ref, tile_ref, column_ref, out_ref):
        out_ref[...] = column_ref[within_column(mine_ref[tile_ref[0]])]

    return on_scalars(body, (mine, tile), (column,), (88, 640))


def on_scalars(body, scalars, arrays, shape):
    return pl.pallas_call(
        body,
        in_specs=[pl.BlockSpec(memory_space=pltpu.SMEM)] * len(scalars)
        + [pl.BlockSpec(memory_space=pltpu.VMEM)] * len(arrays),
        out_specs=pl.BlockSpec(memory_space=pltpu.VMEM),
        out_shape=jax.ShapeDtypeStruct(shape, BF16),
        compiler_params=pltpu.CompilerParams(vmem_limit_bytes=16 << 20),
    )(*scalars, *arrays)


def bases_of_tile(row, rows, four):
    mine = rows[0]
    v_part = exchange(choose_v(row, rows, lax.axis_index("mp")[None]), "mp")
    both = choose_both(row, v_part, mine)
    column = exchange(both, COLUMN)
    column, four = lax.optimization_barrier((column, four))
    one = choose_one(column, mine, lax.axis_index("yj")[None])
    whole = lax.all_gather(one[None], ROW, axis=0, tiled=True)
    u_tile = whole[:, :40].reshape(640, 640)
    v_tile = whole[:, 40:80].reshape(640, 640)
    ei = jnp.sum(whole[0, 80:82].astype(F32), axis=0)
    eo = jnp.sum(whole[0, 82:84].astype(F32), axis=0)
    return four, u_tile, v_tile, ei, eo


def shards(inputs, out_grads, doc_lengths, owners, basis_in, basis_out, eig_in, eig_out):
    sent = rows_sent(basis_in, basis_out, eig_in[0], eig_out[0])
    row, rows, parts = swapped(inputs, out_grads, owners[0], doc_lengths[0], sent)
    four, u, v, ei, eo = bases_of_tile(row, rows, row_sums(parts))
    gt = tile_of_gradient(four)
    first = (lax.axis_index(DP) % 32) * 20
    v_own = lax.dynamic_slice_in_dim(v, first.astype(jnp.uint32), 20, 0)
    rotated = jnp.dot(gt, u, preferred_element_type=F32).astype(BF16)
    twice = lax.dot_general(v, rotated, (((0,), (0,)), ((), ())), preferred_element_type=F32)
    scaled = (twice / (eo[:, None] * ei[None, :] + DAMPING)).astype(BF16)
    back = jnp.dot(v_own, scaled, preferred_element_type=F32).astype(BF16)
    out = lax.dot_general(back, u, (((1,), (1,)), ((), ())), preferred_element_type=F32)
    return out.astype(BF16).T


def solution(mesh):
    fine = Mesh(mesh.devices.reshape(SPLIT), AXES)
    split = P(DP, "mp")
    placed = (split, split, P(DP, None), P("mp", None), split, split, split, split)
    return jax.shard_map(
        shards, mesh=fine, in_specs=placed, out_specs=P("mp", DP), check_vma=False
    )
```

```python
import jax
import jax.numpy as jnp
from jax import lax
from jax.experimental import pallas as pl
from jax.experimental.pallas import tpu as pltpu
from jax.sharding import Mesh
from jax.sharding import PartitionSpec as P

DAMPING = 0.1
SPLIT = (4, 2, 4, 2, 2, 4)
AXES = ("yj", "yh", "x", "zl", "c", "mp")
DP = AXES[:5]
ROW = ("yh", "x", "c")
COLUMN = ("yj", "zl")
F32 = jnp.float32
BF16 = jnp.bfloat16


def token_weights(lengths, row_count, replicas):
    ends = jnp.cumsum(lengths)
    starts = ends - lengths
    positions = jnp.arange(row_count, dtype=jnp.int32)
    inside = (positions[:, None] >= starts[None, :]) & (positions[:, None] < ends[None, :])
    per_row = jnp.sum(jnp.where(inside, lengths[None, :], 0), axis=1)
    return 1.0 / (replicas * per_row.astype(F32))


def exchange(x, axes):
    return lax.all_to_all(x, axes, split_axis=0, concat_axis=0, tiled=True)


def pool(x):
    return lax.all_gather(x, "c", axis=0, tiled=True)


def by_block(entries):
    z = lax.axis_index("mp")
    a, b, c, d = entries
    low, high = z % 2 == 1, z // 2 == 1
    a, b = jnp.where(low, b, a), jnp.where(low, a, b)
    c, d = jnp.where(low, d, c), jnp.where(low, c, d)
    a, c = jnp.where(high, c, a), jnp.where(high, a, c)
    b, d = jnp.where(high, d, b), jnp.where(high, b, d)
    return [a, b, c, d]


def two_terms(v):
    high = lax.reduce_precision(v, 8, 7)
    return jnp.stack([high.astype(BF16), (v - high).astype(BF16)])


def rows_sent(u, v, ei, eo):
    small = jnp.concatenate([two_terms(ei), two_terms(eo), jnp.zeros((4, 640), BF16)])
    small = jnp.broadcast_to(small[None], (16, 8, 640))
    return jnp.concatenate([u.reshape(16, 40, 640), v.reshape(16, 40, 640), small], axis=1)


def products(xs, gs):
    def body(x_ref, x_next_ref, g_ref, g_across_ref, out_ref):
        pairs = [(x, g) for x in (x_ref, x_next_ref) for g in (g_ref, g_across_ref)]
        for i, (x, g) in enumerate(pairs):
            whole = lax.dot_general(
                g[...], x[...], (((0,), (0,)), ((), ())), preferred_element_type=F32
            ).astype(BF16)
            for place in range(4):
                out_ref[place, i] = whole[place * 80 : place * 80 + 80]

    return on_scalars(body, (), (*xs, *gs), (4, 4, 80, 640))


def shift(x, distance):
    return lax.ppermute(x, "mp", [(i, i ^ distance) for i in range(4)])


def first_phase(inputs, out_grads, owners, lengths, sent):
    row = exchange(sent, ROW)
    weights = token_weights(lengths, inputs.shape[0], lax.axis_size(DP))[:, None]
    x = (inputs.astype(F32) * weights).astype(BF16)
    x_next = shift(x, 1)
    g = pool(out_grads)
    g = jnp.where(lax.axis_index("c") == 0, g[:, :320], g[:, 320:])
    g_across = shift(g, 3)
    x = pool(x)
    owners, x, g = lax.optimization_barrier((owners, x, g))
    rows = jnp.stack([owners] + [shift(owners, d) for d in (1, 2, 3)])
    row, rows, x, x_next, g, g_across = lax.optimization_barrier(
        (row, rows, x, x_next, g, g_across)
    )
    return row, rows, products((x, pool(x_next)), (g, g_across))


def row_of_gradient(summed):
    back = shift(summed[2:], 1)
    return jnp.stack(by_block([summed[0], back[0], back[1], summed[1]]))


def tile_of_gradient(four):
    received = exchange(four.reshape(16, 20, 640), ("yj", "yh", "zl"))
    piece = jnp.sum(received.astype(F32), axis=0).astype(BF16)
    spread = exchange(jnp.broadcast_to(piece[None], (16, 20, 640)), ("x", "yh", "zl"))
    return pool(spread.reshape(320, 640))


def within_row(owner):
    return ((owner >> 4) & 1) * 8 + ((owner >> 2) & 3) * 2 + (owner & 1)


def within_column(owner):
    return (owner >> 5) * 2 + ((owner >> 1) & 1)


def choose_v(row, rows, z):
    def body(rows_ref, z_ref, row_ref, out_ref):
        here = z_ref[0]
        for m in range(4):
            source = within_row(rows_ref[(here ^ m) * 4 + here])
            out_ref[m] = row_ref[source, 40:88, :]

    return on_scalars(body, (rows.reshape(16), z), (row,), (4, 48, 640))


def choose_both(row, v_part, mine):
    def body(mine_ref, row_ref, v_ref, out_ref):
        for j in range(4):
            source = within_row(mine_ref[j])
            for half in range(2):
                out_ref[2 * j + half, 0:40, :] = row_ref[source, 0:40, :]
                out_ref[2 * j + half, 40:80, :] = v_ref[j, 0:40, :]
                out_ref[2 * j + half, 80:82, :] = row_ref[source, 80:82, :]
                out_ref[2 * j + half, 82:88, :] = v_ref[j, 42:48, :]

    return on_scalars(body, (mine,), (row, v_part), (8, 88, 640))


def choose_one(column, mine, tile):
    def body(mine_ref, tile_ref, column_ref, out_ref):
        out_ref[...] = column_ref[within_column(mine_ref[tile_ref[0]])]

    return on_scalars(body, (mine, tile), (column,), (88, 640))


def on_scalars(body, scalars, arrays, shape):
    return pl.pallas_call(
        body,
        in_specs=[pl.BlockSpec(memory_space=pltpu.SMEM)] * len(scalars)
        + [pl.BlockSpec(memory_space=pltpu.VMEM)] * len(arrays),
        out_specs=pl.BlockSpec(memory_space=pltpu.VMEM),
        out_shape=jax.ShapeDtypeStruct(shape, BF16),
        compiler_params=pltpu.CompilerParams(vmem_limit_bytes=16 << 20),
    )(*scalars, *arrays)


def bases_of_tile(row, rows, summed):
    mine = rows[0]
    v_part = exchange(choose_v(row, rows, lax.axis_index("mp")[None]), "mp")
    both = choose_both(row, v_part, mine)
    column = exchange(both, COLUMN)
    column, four = lax.optimization_barrier((column, row_of_gradient(summed)))
    one = choose_one(column, mine, lax.axis_index("yj")[None])
    return four, lax.all_gather(one[None], ROW, axis=0, tiled=True)


def precondition(gt, bases, first):
    def body(first_ref, gt_ref, bases_ref, out_ref, u_ref, v_ref):
        for b in range(16):
            u_ref[b * 40 : b * 40 + 40, :] = bases_ref[b, 0:40, :]
            v_ref[b * 40 : b * 40 + 40, :] = bases_ref[b, 40:80, :]
        small = bases_ref[0, 80:84, :].astype(F32)
        ei = small[0:1] + small[1:2]
        eo = small[2:3] + small[3:4]
        u = u_ref[...]
        v = v_ref[...]
        at = lax.broadcasted_iota(jnp.int32, (24, 640), 1) - first_ref[0]
        own = (at == lax.broadcasted_iota(jnp.int32, (24, 640), 0)).astype(F32).astype(BF16)
        v_own = jnp.dot(own, v, preferred_element_type=F32).astype(BF16)
        rotated = jnp.dot(gt_ref[...], u, preferred_element_type=F32).astype(BF16)
        twice = lax.dot_general(
            rotated, v, (((0,), (0,)), ((), ())), preferred_element_type=F32
        )
        scaled = (twice / (ei.T * eo + DAMPING)).astype(BF16)
        back = lax.dot_general(
            v_own, scaled, (((1,), (1,)), ((), ())), preferred_element_type=F32
        ).astype(BF16)
        out = lax.dot_general(back, u, (((1,), (1,)), ((), ())), preferred_element_type=F32)
        out_ref[...] = out.astype(BF16)

    return pl.pallas_call(
        body,
        in_specs=[pl.BlockSpec(memory_space=pltpu.SMEM)]
        + [pl.BlockSpec(memory_space=pltpu.VMEM)] * 2,
        out_specs=pl.BlockSpec(memory_space=pltpu.VMEM),
        out_shape=jax.ShapeDtypeStruct((24, 640), BF16),
        scratch_shapes=[pltpu.VMEM((640, 640), BF16), pltpu.VMEM((640, 640), BF16)],
        compiler_params=pltpu.CompilerParams(vmem_limit_bytes=24 << 20),
    )(first, gt, bases)


def shards(inputs, out_grads, doc_lengths, owners, basis_in, basis_out, eig_in, eig_out):
    sent = rows_sent(basis_in, basis_out, eig_in[0], eig_out[0])
    row, rows, parts = first_phase(inputs, out_grads, owners[0], doc_lengths[0], sent)
    summed = lax.psum_scatter(parts, "x", scatter_dimension=0, tiled=True)[0]
    four, bases = bases_of_tile(row, rows, summed)
    first = ((lax.axis_index(DP) % 32) * 20)[None]
    return precondition(tile_of_gradient(four), bases, first)[:20].T


def solution(mesh):
    fine = Mesh(mesh.devices.reshape(SPLIT), AXES)
    split = P(DP, "mp")
    placed = (split, split, P(DP, None), P("mp", None), split, split, split, split)
    return jax.shard_map(
        shards, mesh=fine, in_specs=placed, out_specs=P("mp", DP), check_vma=False
    )
```

```python
import jax
import jax.numpy as jnp
from jax import lax
from jax.experimental import pallas as pl
from jax.experimental.pallas import tpu as pltpu
from jax.sharding import Mesh
from jax.sharding import PartitionSpec as P

DAMPING = 0.1
SPLIT = (4, 2, 4, 2, 2, 4)
AXES = ("yj", "yh", "x", "zl", "c", "mp")
DP = AXES[:5]
ROW = ("yh", "x", "c")
F32 = jnp.float32
BF16 = jnp.bfloat16


def token_weights(lengths, row_count, replicas):
    ends = jnp.cumsum(lengths)
    starts = ends - lengths
    positions = jnp.arange(row_count, dtype=jnp.int32)
    inside = (positions[:, None] >= starts[None, :]) & (positions[:, None] < ends[None, :])
    per_row = jnp.sum(jnp.where(inside, lengths[None, :], 0), axis=1)
    return 1.0 / (replicas * per_row.astype(F32))


def exchange(x, axes):
    return lax.all_to_all(x, axes, split_axis=0, concat_axis=0, tiled=True)


def pool(x):
    return lax.all_gather(x, "c", axis=0, tiled=True)


def shift(x, distance, axes="mp"):
    return lax.ppermute(x, axes, [(i, i ^ distance) for i in range(lax.axis_size(axes))])


def sum_over_x(parts):
    parts = [parts[0]] + [shift(parts[d], d, "x") for d in (1, 2, 3)]
    return sum(p.astype(F32) for p in parts).astype(BF16)


def by_block(entries):
    z = lax.axis_index("mp")
    a, b, c, d = entries
    low, high = z % 2 == 1, z // 2 == 1
    a, b = jnp.where(low, b, a), jnp.where(low, a, b)
    c, d = jnp.where(low, d, c), jnp.where(low, c, d)
    a, c = jnp.where(high, c, a), jnp.where(high, a, c)
    b, d = jnp.where(high, d, b), jnp.where(high, b, d)
    return [a, b, c, d]


def two_terms(v):
    high = lax.reduce_precision(v, 8, 7)
    return jnp.stack([high.astype(BF16), (v - high).astype(BF16)])


def rows_sent(u, v, ei, eo):
    small = jnp.concatenate([two_terms(ei), two_terms(eo), jnp.zeros((4, 640), BF16)])
    small = jnp.broadcast_to(small[None], (16, 8, 640))
    return jnp.concatenate([u.reshape(16, 40, 640), v.reshape(16, 40, 640), small], axis=1)


def products(x, g, g_across, place):
    def body(place_ref, x_ref, g_ref, across_ref, *refs):
        whole = refs[4]
        for j, g_of_j in enumerate((g_ref, across_ref)):
            whole[...] = lax.dot_general(
                g_of_j[...], x_ref[...], (((0,), (0,)), ((), ())), preferred_element_type=F32
            )
            for d in range(4):
                first = pl.multiple_of((place_ref[0] ^ d) * 80, 16)
                refs[d][j] = whole[pl.ds(first, 80), :].astype(BF16)

    return pl.pallas_call(
        body,
        in_specs=[pl.BlockSpec(memory_space=pltpu.SMEM)]
        + [pl.BlockSpec(memory_space=pltpu.VMEM)] * 3,
        out_specs=[pl.BlockSpec(memory_space=pltpu.VMEM)] * 4,
        out_shape=[jax.ShapeDtypeStruct((2, 80, 640), BF16)] * 4,
        scratch_shapes=[pltpu.VMEM((320, 640), F32)],
        compiler_params=pltpu.CompilerParams(vmem_limit_bytes=16 << 20),
    )(place, x, g, g_across)


def first_phase(inputs, out_grads, owners, lengths, sent):
    row = exchange(sent, ROW)
    weights = token_weights(lengths, inputs.shape[0], lax.axis_size(DP))[:, None]
    x = (inputs.astype(F32) * weights).astype(BF16)
    x_next = shift(x, 1)
    g = pool(out_grads)
    g = jnp.where(lax.axis_index("c") == 0, g[:, :320], g[:, 320:])
    g_across = shift(g, 3)
    x = pool(x)
    owners, x, g = lax.optimization_barrier((owners, x, g))
    rows = jnp.stack([owners] + [shift(owners, d) for d in (1, 2, 3)])
    row, rows, x, x_next, g, g_across = lax.optimization_barrier(
        (row, rows, x, x_next, g, g_across)
    )
    place = lax.axis_index("x")[None]
    away = products(pool(x_next), g, g_across, place)
    here = products(x, g, g_across, place)
    return row, rows, away, here


def tile_of_gradient(four):
    received = exchange(four.reshape(16, 20, 640), ("yj", "yh", "zl"))
    piece = jnp.sum(received.astype(F32), axis=0).astype(BF16)
    spread = exchange(jnp.broadcast_to(piece[None], (16, 20, 640)), ("x", "yh", "zl"))
    return pool(spread.reshape(320, 640))


def within_row(owner):
    return ((owner >> 4) & 1) * 8 + ((owner >> 2) & 3) * 2 + (owner & 1)


def choose_v(row, rows, z):
    def body(rows_ref, z_ref, row_ref, out_ref):
        here = z_ref[0]
        for m in range(4):
            source = within_row(rows_ref[(here ^ m) * 4 + here])
            out_ref[m] = row_ref[source, 40:88, :]

    return on_scalars(body, (rows.reshape(16), z), (row,), (4, 48, 640))


def choose_both(row, v_part, mine):
    def body(mine_ref, row_ref, v_ref, out_ref):
        for j in range(4):
            source = within_row(mine_ref[j])
            out_ref[j, 0:40, :] = row_ref[source, 0:40, :]
            out_ref[j, 40:80, :] = v_ref[j, 0:40, :]
            out_ref[j, 80:82, :] = row_ref[source, 80:82, :]
            out_ref[j, 82:88, :] = v_ref[j, 42:48, :]

    return on_scalars(body, (mine,), (row, v_part), (4, 88, 640))


def choose_one(column, mine, tile):
    def body(mine_ref, tile_ref, column_ref, out_ref):
        out_ref[...] = column_ref[mine_ref[tile_ref[0]] >> 5]

    return on_scalars(body, (mine, tile), (column,), (88, 640))


def choose_pair(parts, mine, tile, yh, zl):
    def body(mine_ref, tile_ref, yh_ref, zl_ref, *refs):
        out_ref = refs[4]
        here, other = yh_ref[0], 1 - yh_ref[0]
        same = ((mine_ref[tile_ref[0]] >> 1) & 1) == zl_ref[0]

        @pl.when(same)
        def _():
            out_ref[here] = refs[0][...]
            out_ref[other] = refs[2][...]

        @pl.when(jnp.logical_not(same))
        def _():
            out_ref[here] = refs[1][...]
            out_ref[other] = refs[3][...]

    return on_scalars(body, (mine, tile, yh, zl), parts, (2, 88, 640))


def on_scalars(body, scalars, arrays, shape):
    return pl.pallas_call(
        body,
        in_specs=[pl.BlockSpec(memory_space=pltpu.SMEM)] * len(scalars)
        + [pl.BlockSpec(memory_space=pltpu.VMEM)] * len(arrays),
        out_specs=pl.BlockSpec(memory_space=pltpu.VMEM),
        out_shape=jax.ShapeDtypeStruct(shape, BF16),
        compiler_params=pltpu.CompilerParams(vmem_limit_bytes=16 << 20),
    )(*scalars, *arrays)


def second_phase(row, rows, away, here):
    mine = rows[0]
    v_part = exchange(choose_v(row, rows, lax.axis_index("mp")[None]), "mp")
    v_part, away = lax.optimization_barrier((v_part, away))
    column = exchange(choose_both(row, v_part, mine), "yj")
    column, away = lax.optimization_barrier((column, sum_over_x(away)))
    back = shift(away, 1)
    here = sum_over_x(here)
    four = jnp.stack(by_block([here[0], back[0], back[1], here[1]]))
    tile, yh, zl = [lax.axis_index(a)[None] for a in ("yj", "yh", "zl")]
    one = choose_one(column, mine, tile)
    parts = [one] + [shift(one, d, ("yh", "zl")) for d in (1, 2, 3)]
    four, parts = lax.optimization_barrier((four, parts))
    pair = choose_pair(parts, mine, tile, yh, zl)
    return four, jnp.stack([pair] + [shift(pair, d, "x") for d in (1, 2, 3)])


def precondition(gt, near, far, place, core, first):
    def body(place_ref, core_ref, first_ref, gt_ref, near_ref, far_ref, out_ref, u_ref, v_ref):
        for e, ref in enumerate((near_ref, far_ref)):
            for d in range(4):
                for h in range(2):
                    at = h * 8 + (place_ref[0] ^ d) * 2 + (core_ref[0] ^ e)
                    rows = pl.ds(pl.multiple_of(at * 40, 8), 40)
                    part = ref[d, h].astype(F32)
                    u_ref[rows, :] = part[0:40]
                    v_ref[rows, :] = part[40:80]
        small = near_ref[0, 0, 80:84, :].astype(F32)
        ei = small[0:1] + small[1:2]
        eo = small[2:3] + small[3:4]
        u = u_ref[...].astype(BF16)
        v = v_ref[...].astype(BF16)
        at = lax.broadcasted_iota(jnp.int32, (24, 640), 1) - first_ref[0]
        own = (at == lax.broadcasted_iota(jnp.int32, (24, 640), 0)).astype(F32).astype(BF16)
        v_own = jnp.dot(own, v, preferred_element_type=F32).astype(BF16)
        rotated = jnp.dot(gt_ref[...], u, preferred_element_type=F32).astype(BF16)
        twice = lax.dot_general(
            rotated, v, (((0,), (0,)), ((), ())), preferred_element_type=F32
        )
        scaled = (twice / (ei.T * eo + DAMPING)).astype(BF16)
        back = lax.dot_general(
            v_own, scaled, (((1,), (1,)), ((), ())), preferred_element_type=F32
        ).astype(BF16)
        out = lax.dot_general(back, u, (((1,), (1,)), ((), ())), preferred_element_type=F32)
        out_ref[...] = out.astype(BF16)

    return pl.pallas_call(
        body,
        in_specs=[pl.BlockSpec(memory_space=pltpu.SMEM)] * 3
        + [pl.BlockSpec(memory_space=pltpu.VMEM)] * 3,
        out_specs=pl.BlockSpec(memory_space=pltpu.VMEM),
        out_shape=jax.ShapeDtypeStruct((24, 640), BF16),
        scratch_shapes=[pltpu.VMEM((640, 640), F32)] * 2,
        compiler_params=pltpu.CompilerParams(vmem_limit_bytes=24 << 20),
    )(place, core, first, gt, near, far)


def shards(inputs, out_grads, doc_lengths, owners, basis_in, basis_out, eig_in, eig_out):
    sent = rows_sent(basis_in, basis_out, eig_in[0], eig_out[0])
    first = first_phase(inputs, out_grads, owners[0], doc_lengths[0], sent)
    four, near = second_phase(*first)
    far = lax.ppermute(near, "c", [(0, 1), (1, 0)])
    place, core = lax.axis_index("x")[None], lax.axis_index("c")[None]
    first = ((lax.axis_index(DP) % 32) * 20)[None]
    return precondition(tile_of_gradient(four), near, far, place, core, first)[:20].T


def solution(mesh):
    fine = Mesh(mesh.devices.reshape(SPLIT), AXES)
    split = P(DP, "mp")
    placed = (split, split, P(DP, None), P("mp", None), split, split, split, split)
    return jax.shard_map(
        shards, mesh=fine, in_specs=placed, out_specs=P("mp", DP), check_vma=False
    )
```

```python
import jax
import jax.numpy as jnp
from jax import lax
from jax.experimental import pallas as pl
from jax.experimental.pallas import tpu as pltpu
from jax.sharding import Mesh
from jax.sharding import PartitionSpec as P

DAMPING = 0.1
SPLIT = (4, 2, 4, 2, 2, 4)
AXES = ("yj", "yh", "x", "zl", "c", "mp")
DP = AXES[:5]
ROW = ("yh", "x", "c")
F32 = jnp.float32
BF16 = jnp.bfloat16


def token_weights(lengths, row_count, replicas):
    ends = jnp.cumsum(lengths)
    starts = ends - lengths
    positions = jnp.arange(row_count, dtype=jnp.int32)
    inside = (positions[:, None] >= starts[None, :]) & (positions[:, None] < ends[None, :])
    per_row = jnp.sum(jnp.where(inside, lengths[None, :], 0), axis=1)
    return 1.0 / (replicas * per_row.astype(F32))


def exchange(x, axes):
    return lax.all_to_all(x, axes, split_axis=0, concat_axis=0, tiled=True)


def pool(x):
    return lax.all_gather(x, "c", axis=0, tiled=True)


def shift(x, distance, axes="mp"):
    return lax.ppermute(x, axes, [(i, i ^ distance) for i in range(lax.axis_size(axes))])


def sum_over_x(parts):
    parts = [parts[0]] + [shift(parts[d], d, "x") for d in (1, 2, 3)]
    return sum(p.astype(F32) for p in parts).astype(BF16)


def by_block(entries):
    z = lax.axis_index("mp")
    a, b, c, d = entries
    low, high = z % 2 == 1, z // 2 == 1
    a, b = jnp.where(low, b, a), jnp.where(low, a, b)
    c, d = jnp.where(low, d, c), jnp.where(low, c, d)
    a, c = jnp.where(high, c, a), jnp.where(high, a, c)
    b, d = jnp.where(high, d, b), jnp.where(high, b, d)
    return [a, b, c, d]


def two_terms(v):
    high = lax.reduce_precision(v, 8, 7)
    return jnp.stack([high.astype(BF16), (v - high).astype(BF16)])


def rows_sent(u, v, ei, eo):
    small = jnp.concatenate([two_terms(ei), two_terms(eo), jnp.zeros((4, 640), BF16)])
    small = jnp.broadcast_to(small[None], (16, 8, 640))
    return jnp.concatenate([u.reshape(16, 40, 640), v.reshape(16, 40, 640), small], axis=1)


def products(x, g, g_across, place):
    def body(place_ref, x_ref, g_ref, across_ref, *refs):
        whole = refs[4]
        for j, g_of_j in enumerate((g_ref, across_ref)):
            whole[...] = lax.dot_general(
                g_of_j[...], x_ref[...], (((0,), (0,)), ((), ())), preferred_element_type=F32
            )
            for d in range(4):
                first = pl.multiple_of((place_ref[0] ^ d) * 80, 16)
                refs[d][j] = whole[pl.ds(first, 80), :].astype(BF16)

    return pl.pallas_call(
        body,
        in_specs=[pl.BlockSpec(memory_space=pltpu.SMEM)]
        + [pl.BlockSpec(memory_space=pltpu.VMEM)] * 3,
        out_specs=[pl.BlockSpec(memory_space=pltpu.VMEM)] * 4,
        out_shape=[jax.ShapeDtypeStruct((2, 80, 640), BF16)] * 4,
        scratch_shapes=[pltpu.VMEM((320, 640), F32)],
        compiler_params=pltpu.CompilerParams(vmem_limit_bytes=16 << 20),
    )(place, x, g, g_across)


def first_phase(inputs, out_grads, owners, lengths, sent):
    row = exchange(sent, ROW)
    weights = token_weights(lengths, inputs.shape[0], lax.axis_size(DP))[:, None]
    x = (inputs.astype(F32) * weights).astype(BF16)
    x_next = shift(x, 1)
    g = pool(out_grads)
    g = jnp.where(lax.axis_index("c") == 0, g[:, :320], g[:, 320:])
    g_across = shift(g, 3)
    x = pool(x)
    owners, x, g = lax.optimization_barrier((owners, x, g))
    rows = jnp.stack([owners] + [shift(owners, d) for d in (1, 2, 3)])
    row, rows, x, x_next, g, g_across = lax.optimization_barrier(
        (row, rows, x, x_next, g, g_across)
    )
    place = lax.axis_index("x")[None]
    away = products(pool(x_next), g, g_across, place)
    here = products(x, g, g_across, place)
    return row, rows, away, here


def tile_of_gradient(four):
    received = exchange(four.reshape(16, 20, 640), ("yj", "yh", "zl"))
    piece = jnp.sum(received.astype(F32), axis=0).astype(BF16)
    spread = exchange(jnp.broadcast_to(piece[None], (16, 20, 640)), ("x", "yh", "zl"))
    return pool(spread.reshape(320, 640))


def within_row(owner):
    return ((owner >> 4) & 1) * 8 + ((owner >> 2) & 3) * 2 + (owner & 1)


def choose_v(row, rows, z):
    def body(rows_ref, z_ref, row_ref, out_ref):
        here = z_ref[0]
        for m in range(4):
            source = within_row(rows_ref[(here ^ m) * 4 + here])
            out_ref[m] = row_ref[source, 40:88, :]

    return on_scalars(body, (rows.reshape(16), z), (row,), (4, 48, 640))


def choose_both(row, v_part, mine):
    def body(mine_ref, row_ref, v_ref, out_ref):
        for j in range(4):
            source = within_row(mine_ref[j])
            for half in range(2):
                out_ref[2 * j + half, 0:40, :] = row_ref[source, 0:40, :]
                out_ref[2 * j + half, 40:80, :] = v_ref[j, 0:40, :]
                out_ref[2 * j + half, 80:82, :] = row_ref[source, 80:82, :]
                out_ref[2 * j + half, 82:88, :] = v_ref[j, 42:48, :]

    return on_scalars(body, (mine,), (row, v_part), (8, 88, 640))


def choose_pair(column, mine, tile):
    def body(mine_ref, tile_ref, column_ref, out_ref):
        source = mine_ref[tile_ref[0]] >> 5
        for half in range(2):
            out_ref[half] = column_ref[2 * source + half]

    return on_scalars(body, (mine, tile), (column,), (2, 88, 640))


def choose_near(pair, other, mine, tile, zl):
    def body(mine_ref, tile_ref, zl_ref, pair_ref, other_ref, out_ref):
        same = ((mine_ref[tile_ref[0]] >> 1) & 1) == zl_ref[0]

        @pl.when(same)
        def _():
            out_ref[...] = pair_ref[...]

        @pl.when(jnp.logical_not(same))
        def _():
            out_ref[...] = other_ref[...]

    return on_scalars(body, (mine, tile, zl), (pair, other), (2, 88, 640))


def on_scalars(body, scalars, arrays, shape):
    return pl.pallas_call(
        body,
        in_specs=[pl.BlockSpec(memory_space=pltpu.SMEM)] * len(scalars)
        + [pl.BlockSpec(memory_space=pltpu.VMEM)] * len(arrays),
        out_specs=pl.BlockSpec(memory_space=pltpu.VMEM),
        out_shape=jax.ShapeDtypeStruct(shape, BF16),
        compiler_params=pltpu.CompilerParams(vmem_limit_bytes=16 << 20),
    )(*scalars, *arrays)


def second_phase(row, rows, away, here):
    mine = rows[0]
    v_part = exchange(choose_v(row, rows, lax.axis_index("mp")[None]), "mp")
    away = list(away)
    v_part, away[0] = lax.optimization_barrier((v_part, away[0]))
    column = exchange(choose_both(row, v_part, mine), ("yj", "yh"))
    column, away = lax.optimization_barrier((column, sum_over_x(away)))
    back = shift(away, 1)
    here = sum_over_x(here)
    four = jnp.stack(by_block([here[0], back[0], back[1], here[1]]))
    tile, zl = [lax.axis_index(a)[None] for a in ("yj", "zl")]
    pair = choose_pair(column, mine, tile)
    other = shift(pair, 1, "zl")
    four, other = lax.optimization_barrier((four, other))
    pair = choose_near(pair, other, mine, tile, zl)
    return four, jnp.stack([pair] + [shift(pair, d, "x") for d in (1, 2, 3)])


def precondition(gt, near, far, place, core, first):
    def body(place_ref, core_ref, first_ref, gt_ref, near_ref, far_ref, out_ref, u_ref, v_ref):
        for e, ref in enumerate((near_ref, far_ref)):
            for d in range(4):
                for h in range(2):
                    at = h * 8 + (place_ref[0] ^ d) * 2 + (core_ref[0] ^ e)
                    rows = pl.ds(pl.multiple_of(at * 40, 8), 40)
                    part = ref[d, h].astype(F32)
                    u_ref[rows, :] = part[0:40]
                    v_ref[rows, :] = part[40:80]
        small = near_ref[0, 0, 80:84, :].astype(F32)
        ei = small[0:1] + small[1:2]
        eo = small[2:3] + small[3:4]
        u = u_ref[...].astype(BF16)
        v = v_ref[...].astype(BF16)
        at = lax.broadcasted_iota(jnp.int32, (24, 640), 1) - first_ref[0]
        own = (at == lax.broadcasted_iota(jnp.int32, (24, 640), 0)).astype(F32).astype(BF16)
        v_own = jnp.dot(own, v, preferred_element_type=F32).astype(BF16)
        rotated = jnp.dot(gt_ref[...], u, preferred_element_type=F32).astype(BF16)
        twice = lax.dot_general(
            rotated, v, (((0,), (0,)), ((), ())), preferred_element_type=F32
        )
        scaled = (twice / (ei.T * eo + DAMPING)).astype(BF16)
        back = lax.dot_general(
            v_own, scaled, (((1,), (1,)), ((), ())), preferred_element_type=F32
        ).astype(BF16)
        out = lax.dot_general(back, u, (((1,), (1,)), ((), ())), preferred_element_type=F32)
        out_ref[...] = out.astype(BF16)

    return pl.pallas_call(
        body,
        in_specs=[pl.BlockSpec(memory_space=pltpu.SMEM)] * 3
        + [pl.BlockSpec(memory_space=pltpu.VMEM)] * 3,
        out_specs=pl.BlockSpec(memory_space=pltpu.VMEM),
        out_shape=jax.ShapeDtypeStruct((24, 640), BF16),
        scratch_shapes=[pltpu.VMEM((640, 640), F32)] * 2,
        compiler_params=pltpu.CompilerParams(vmem_limit_bytes=24 << 20),
    )(place, core, first, gt, near, far)


def shards(inputs, out_grads, doc_lengths, owners, basis_in, basis_out, eig_in, eig_out):
    sent = rows_sent(basis_in, basis_out, eig_in[0], eig_out[0])
    first = first_phase(inputs, out_grads, owners[0], doc_lengths[0], sent)
    four, near = second_phase(*first)
    far = lax.ppermute(near, "c", [(0, 1), (1, 0)])
    place, core = lax.axis_index("x")[None], lax.axis_index("c")[None]
    first = ((lax.axis_index(DP) % 32) * 20)[None]
    return precondition(tile_of_gradient(four), near, far, place, core, first)[:20].T


def solution(mesh):
    fine = Mesh(mesh.devices.reshape(SPLIT), AXES)
    split = P(DP, "mp")
    placed = (split, split, P(DP, None), P("mp", None), split, split, split, split)
    return jax.shard_map(
        shards, mesh=fine, in_specs=placed, out_specs=P("mp", DP), check_vma=False
    )
```

```python
import jax
import jax.numpy as jnp
from jax import lax
from jax.experimental import pallas as pl
from jax.experimental.pallas import tpu as pltpu
from jax.sharding import Mesh
from jax.sharding import PartitionSpec as P

DAMPING = 0.1
SPLIT = (4, 2, 4, 2, 2, 4)
AXES = ("yj", "yh", "x", "zl", "c", "mp")
DP = AXES[:5]
ROW = ("yh", "x", "c")
F32 = jnp.float32
BF16 = jnp.bfloat16


def token_weights(lengths, row_count, replicas):
    ends = jnp.cumsum(lengths)
    starts = ends - lengths
    positions = jnp.arange(row_count, dtype=jnp.int32)
    inside = (positions[:, None] >= starts[None, :]) & (positions[:, None] < ends[None, :])
    per_row = jnp.sum(jnp.where(inside, lengths[None, :], 0), axis=1)
    return 1.0 / (replicas * per_row.astype(F32))


def exchange(x, axes):
    return lax.all_to_all(x, axes, split_axis=0, concat_axis=0, tiled=True)


def pool(x):
    return lax.all_gather(x, "c", axis=0, tiled=True)


def shift(x, distance, axes="mp"):
    return lax.ppermute(x, axes, [(i, i ^ distance) for i in range(lax.axis_size(axes))])


def sum_over_x(parts):
    parts = [parts[0]] + [shift(parts[d], d, "x") for d in (1, 2, 3)]
    return sum(p.astype(F32) for p in parts).astype(BF16)


def by_block(entries):
    z = lax.axis_index("mp")
    a, b, c, d = entries
    low, high = z % 2 == 1, z // 2 == 1
    a, b = jnp.where(low, b, a), jnp.where(low, a, b)
    c, d = jnp.where(low, d, c), jnp.where(low, c, d)
    a, c = jnp.where(high, c, a), jnp.where(high, a, c)
    b, d = jnp.where(high, d, b), jnp.where(high, b, d)
    return [a, b, c, d]


def two_terms(v):
    high = lax.reduce_precision(v, 8, 7)
    return jnp.stack([high.astype(BF16), (v - high).astype(BF16)])


def rows_sent(u, v, ei, eo):
    small = jnp.concatenate([two_terms(ei), two_terms(eo), jnp.zeros((4, 640), BF16)])
    small = jnp.broadcast_to(small[None], (16, 8, 640))
    return jnp.concatenate([u.reshape(16, 40, 640), v.reshape(16, 40, 640), small], axis=1)


def products(x, g, g_across, place):
    def body(place_ref, x_ref, g_ref, across_ref, *refs):
        whole = refs[4]
        for j, g_of_j in enumerate((g_ref, across_ref)):
            whole[...] = lax.dot_general(
                g_of_j[...], x_ref[...], (((0,), (0,)), ((), ())), preferred_element_type=F32
            )
            for d in range(4):
                first = pl.multiple_of((place_ref[0] ^ d) * 80, 16)
                refs[d][j] = whole[pl.ds(first, 80), :].astype(BF16)

    return pl.pallas_call(
        body,
        in_specs=[pl.BlockSpec(memory_space=pltpu.SMEM)]
        + [pl.BlockSpec(memory_space=pltpu.VMEM)] * 3,
        out_specs=[pl.BlockSpec(memory_space=pltpu.VMEM)] * 4,
        out_shape=[jax.ShapeDtypeStruct((2, 80, 640), BF16)] * 4,
        scratch_shapes=[pltpu.VMEM((320, 640), F32)],
        compiler_params=pltpu.CompilerParams(vmem_limit_bytes=16 << 20),
    )(place, x, g, g_across)


def first_phase(inputs, out_grads, owners, lengths, sent):
    row = exchange(sent, ROW)
    weights = token_weights(lengths, inputs.shape[0], lax.axis_size(DP))[:, None]
    x = (inputs.astype(F32) * weights).astype(BF16)
    x_next = shift(x, 1)
    g = pool(out_grads)
    g = jnp.where(lax.axis_index("c") == 0, g[:, :320], g[:, 320:])
    g_across = shift(g, 3)
    x = pool(x)
    owners, x, g = lax.optimization_barrier((owners, x, g))
    rows = jnp.stack([owners] + [shift(owners, d) for d in (1, 2, 3)])
    row, rows, x, x_next, g, g_across = lax.optimization_barrier(
        (row, rows, x, x_next, g, g_across)
    )
    place = lax.axis_index("x")[None]
    away = products(pool(x_next), g, g_across, place)
    here = products(x, g, g_across, place)
    return row, rows, away, here


def sum_for_all(received):
    def body(received_ref, out_ref):
        total = jnp.zeros((20, 640), F32)
        for i in range(16):
            total += received_ref[i].astype(F32)
        piece = total.astype(BF16)
        for i in range(16):
            out_ref[i] = piece

    return on_scalars(body, (), (received,), (16, 20, 640))


def tile_of_gradient(four):
    received = exchange(four.reshape(16, 20, 640), ("yj", "yh", "zl"))
    spread = exchange(sum_for_all(received), ("x", "yh", "zl"))
    return pool(spread.reshape(320, 640))


def within_row(owner):
    return ((owner >> 4) & 1) * 8 + ((owner >> 2) & 3) * 2 + (owner & 1)


def choose_v(row, rows, z):
    def body(rows_ref, z_ref, row_ref, out_ref):
        here = z_ref[0]
        for m in range(4):
            source = within_row(rows_ref[(here ^ m) * 4 + here])
            out_ref[m] = row_ref[source, 40:88, :]

    return on_scalars(body, (rows.reshape(16), z), (row,), (4, 48, 640))


def choose_both(row, v_part, mine):
    def body(mine_ref, row_ref, v_ref, out_ref):
        for j in range(4):
            source = within_row(mine_ref[j])
            for half in range(2):
                out_ref[2 * j + half, 0:40, :] = row_ref[source, 0:40, :]
                out_ref[2 * j + half, 40:80, :] = v_ref[j, 0:40, :]
                out_ref[2 * j + half, 80:82, :] = row_ref[source, 80:82, :]
                out_ref[2 * j + half, 82:88, :] = v_ref[j, 42:48, :]

    return on_scalars(body, (mine,), (row, v_part), (8, 88, 640))


def choose_pair(column, mine, tile):
    def body(mine_ref, tile_ref, column_ref, out_ref):
        source = mine_ref[tile_ref[0]] >> 5
        for half in range(2):
            out_ref[half] = column_ref[2 * source + half]

    return on_scalars(body, (mine, tile), (column,), (2, 88, 640))


def choose_near(pair, other, mine, tile, zl):
    def body(mine_ref, tile_ref, zl_ref, pair_ref, other_ref, out_ref):
        same = ((mine_ref[tile_ref[0]] >> 1) & 1) == zl_ref[0]

        @pl.when(same)
        def _():
            out_ref[...] = pair_ref[...]

        @pl.when(jnp.logical_not(same))
        def _():
            out_ref[...] = other_ref[...]

    return on_scalars(body, (mine, tile, zl), (pair, other), (2, 88, 640))


def on_scalars(body, scalars, arrays, shape):
    return pl.pallas_call(
        body,
        in_specs=[pl.BlockSpec(memory_space=pltpu.SMEM)] * len(scalars)
        + [pl.BlockSpec(memory_space=pltpu.VMEM)] * len(arrays),
        out_specs=pl.BlockSpec(memory_space=pltpu.VMEM),
        out_shape=jax.ShapeDtypeStruct(shape, BF16),
        compiler_params=pltpu.CompilerParams(vmem_limit_bytes=16 << 20),
    )(*scalars, *arrays)


def second_phase(row, rows, away, here):
    mine = rows[0]
    v_part = exchange(choose_v(row, rows, lax.axis_index("mp")[None]), "mp")
    away = list(away)
    v_part, away[0] = lax.optimization_barrier((v_part, away[0]))
    column = exchange(choose_both(row, v_part, mine), ("yj", "yh"))
    column, away = lax.optimization_barrier((column, sum_over_x(away)))
    back = shift(away, 1)
    here = sum_over_x(here)
    four = jnp.stack(by_block([here[0], back[0], back[1], here[1]]))
    tile, zl = [lax.axis_index(a)[None] for a in ("yj", "zl")]
    pair = choose_pair(column, mine, tile)
    other = shift(pair, 1, "zl")
    four, other = lax.optimization_barrier((four, other))
    pair = choose_near(pair, other, mine, tile, zl)
    return four, jnp.stack([pair] + [shift(pair, d, "x") for d in (1, 2, 3)])


def precondition(gt, near, far, place, core, first):
    def body(place_ref, core_ref, first_ref, gt_ref, near_ref, far_ref, out_ref, u_ref, v_ref):
        for e, ref in enumerate((near_ref, far_ref)):
            for d in range(4):
                for h in range(2):
                    at = h * 8 + (place_ref[0] ^ d) * 2 + (core_ref[0] ^ e)
                    rows = pl.ds(pl.multiple_of(at * 40, 8), 40)
                    part = ref[d, h].astype(F32)
                    u_ref[rows, :] = part[0:40]
                    v_ref[rows, :] = part[40:80]
        small = near_ref[0, 0, 80:84, :].astype(F32)
        ei = small[0:1] + small[1:2]
        eo = small[2:3] + small[3:4]
        u = u_ref[...].astype(BF16)
        v = v_ref[...].astype(BF16)
        at = lax.broadcasted_iota(jnp.int32, (24, 640), 1) - first_ref[0]
        own = (at == lax.broadcasted_iota(jnp.int32, (24, 640), 0)).astype(F32).astype(BF16)
        v_own = jnp.dot(own, v, preferred_element_type=F32).astype(BF16)
        rotated = jnp.dot(gt_ref[...], u, preferred_element_type=F32).astype(BF16)
        twice = lax.dot_general(
            rotated, v, (((0,), (0,)), ((), ())), preferred_element_type=F32
        )
        scaled = (twice / (ei.T * eo + DAMPING)).astype(BF16)
        back = lax.dot_general(
            v_own, scaled, (((1,), (1,)), ((), ())), preferred_element_type=F32
        ).astype(BF16)
        out = lax.dot_general(back, u, (((1,), (1,)), ((), ())), preferred_element_type=F32)
        out_ref[...] = out[0:20].astype(BF16)

    return pl.pallas_call(
        body,
        in_specs=[pl.BlockSpec(memory_space=pltpu.SMEM)] * 3
        + [pl.BlockSpec(memory_space=pltpu.VMEM)] * 3,
        out_specs=pl.BlockSpec(memory_space=pltpu.VMEM),
        out_shape=jax.ShapeDtypeStruct((20, 640), BF16),
        scratch_shapes=[pltpu.VMEM((640, 640), F32)] * 2,
        compiler_params=pltpu.CompilerParams(vmem_limit_bytes=24 << 20),
    )(place, core, first, gt, near, far)


def shards(inputs, out_grads, doc_lengths, owners, basis_in, basis_out, eig_in, eig_out):
    sent = rows_sent(basis_in, basis_out, eig_in[0], eig_out[0])
    first = first_phase(inputs, out_grads, owners[0], doc_lengths[0], sent)
    four, near = second_phase(*first)
    far = lax.ppermute(near, "c", [(0, 1), (1, 0)])
    place, core = lax.axis_index("x")[None], lax.axis_index("c")[None]
    first = ((lax.axis_index(DP) % 32) * 20)[None]
    return precondition(tile_of_gradient(four), near, far, place, core, first).T


def solution(mesh):
    fine = Mesh(mesh.devices.reshape(SPLIT), AXES)
    split = P(DP, "mp")
    placed = (split, split, P(DP, None), P("mp", None), split, split, split, split)
    return jax.shard_map(
        shards, mesh=fine, in_specs=placed, out_specs=P("mp", DP), check_vma=False
    )
```
